768 devices in a mesh: replica: 4 (over z_hi, core), fsdp: 192 (over z_lo, x, y).
Axes of the slice: x: 4, y: 8, z: 12 (z_hi: 2, z_lo: 6; z = z_hi * 6 + z_lo), core: 2. Of those that a mesh axis runs over, the one named last changes fastest.
Arguments:
- tokens: bfloat16 [4, 1536, 4096], P('replica', 'fsdp'), may hold values from -6 to 6
- gate_weight: bfloat16 [4096, 24576], P(None, 'fsdp'), may hold values from -0.09375 to 0.09375
- pseudo_grad: bfloat16 [4, 4096, 24576], P('replica', None, 'fsdp'), may hold values from -0.125 to 0.125
- anchor: float32 [4096, 24576], P('replica', 'fsdp'), may hold values from -0.09375 to 0.09375
- momentum: float32 [4096, 24576], P('replica', 'fsdp'), may hold values from -0.09375 to 0.09375
Outputs:
- new_anchor: float32 [4096, 24576], P('replica', 'fsdp')
- new_momentum: float32 [4096, 24576], P('replica', 'fsdp')
- hidden: bfloat16 [4, 1536, 24576], P('replica', None, 'fsdp')
The draws below stay inside these ranges and needn't reach their ends.
All inputs are finite; a program needn't handle non-finite values.
Results may differ from the reference program's by a relative error of at most 0.015.
Values may be sent and summed in bfloat16 or wider, within the bound.
No kernel may reach another device: no remote copies, remote signals or barrier semaphores. Data moves between devices by JAX's collectives and lax.ppermute only.
A program may use at most 128 MiB of HBM per device.

```python
import jax
import jax.numpy as jnp

DW = 4096
FW = 24576
TOKENS = 1536
N_REPLICA = 4


def with_spikes(values, stream_key, source, target, shards_of, factor):
    def block_of(dim):
        return (jnp.arange(values.shape[dim]) // (values.shape[dim] // shards_of)).reshape((-1,) + (1,) * (values.ndim - 1 - dim))

    one_side = jax.random.permutation(stream_key, shards_of)[block_of(target)]
    second = (block_of(target) + shards_of // 2) % shards_of
    return jnp.where((block_of(source) == one_side) | (block_of(source) == second), factor * values, values)


def block_scale(key, dims, shards, smallest, top_value):
    loudness, own = 1.0, jax.random.fold_in(key, 6)
    for axis_at, blocks in shards:
        draws = jnp.exp(jax.random.uniform(jax.random.fold_in(own, axis_at), (blocks,), jnp.float32, smallest / len(shards), top_value / len(shards)))
        loudness = loudness * jnp.repeat(draws, dims[axis_at] // blocks).reshape([-1 if axis == axis_at else 1 for axis in range(len(dims))])
    return loudness


def centred(own_key, dims, width, bound, shards=(), held_as=jnp.bfloat16):
    result = jax.random.normal(own_key, dims, jnp.float32) * width
    if len(shards) > 0:
        result = block_scale(own_key, dims, shards, -0.22, 0.18) * result
    return jnp.clip(result, min=-bound, max=bound).astype(held_as)


def noise_with(rng, dims, width, reach, shards, heavy, dtype=jnp.bfloat16):
    drawn = width * jax.random.normal(rng, dims, jnp.float32)
    if shards:
        drawn = drawn * block_scale(rng, dims, shards, -0.22, 0.18)
    return jnp.clip(with_spikes(drawn, jax.random.fold_in(rng, 3), *heavy), -reach, reach).astype(dtype)


def setup_inputs(seed: int = 0) -> dict:
    key_of = jax.random.split(jax.random.key(seed), 6)
    return {
        "tokens": centred(key_of[0], (N_REPLICA, TOKENS, DW), 1.0, 6.0, ((0, 4), (1, 192))),
        "gate_weight": centred(key_of[1], (DW, FW), DW ** -0.5, 0.09375, ((1, 192),)),
        "pseudo_grad": noise_with(key_of[2], (N_REPLICA, DW, FW), DW ** -0.5, 0.125, ((0, 4), (2, 192)), (0, 1, 4, 2.0)),
        "anchor": centred(key_of[3], (DW, FW), DW ** -0.5, 0.09375, ((0, 4), (1, 192)), jnp.float32),
        "momentum": centred(key_of[4], (DW, FW), DW ** -0.5, 0.09375, ((0, 4), (1, 192)), jnp.float32),
    }


def reference(tokens, gate_weight, pseudo_grad, anchor, momentum):
    total = jnp.zeros(anchor.shape, jnp.float32)
    for group in range(N_REPLICA):
        total = total + pseudo_grad[group].astype(jnp.float32)
    mean_delta = total / N_REPLICA
    new_momentum = 0.9 * momentum + mean_delta
    new_anchor = anchor - 0.7 * (mean_delta + 0.9 * new_momentum)
    up_weight = new_anchor.astype(jnp.bfloat16)
    outputs = []
    for group in range(N_REPLICA):
        gate = jnp.dot(tokens[group], gate_weight, preferred_element_type=jnp.float32)
        up_part = jnp.dot(tokens[group], up_weight, preferred_element_type=jnp.float32)
        outputs.append((jax.nn.silu(gate) * up_part).astype(jnp.bfloat16))
    return new_anchor, new_momentum, jnp.stack(outputs, 0)
```

```python
import jax
import jax.numpy as jnp
from jax import lax
from jax.sharding import Mesh, PartitionSpec as P

ZH, C, Z, X, Y = 2, 2, 6, 4, 8
AXES = ("zh", "c", "z", "x", "y")
BF, F32 = jnp.bfloat16, jnp.float32


def send(value, move, axis):
    sizes = dict(zip(AXES, (ZH, C, Z, X, Y)))
    return lax.ppermute(value, axis, [(i, move(i)) for i in range(sizes[axis])])


def shift(value, axis, by):
    size = dict(zip(AXES, (ZH, C, Z, X, Y)))[axis]
    return send(value, lambda i: (i + by) % size, axis)


def flip(value, axis):
    return send(value, lambda i: i ^ 1, axis)


def pick(value, axis, at):
    return lax.dynamic_index_in_dim(value, at, axis, keepdims=False)


def roll_to(value, axis, by):
    n = value.shape[axis]
    return lax.dynamic_slice_in_dim(jnp.concatenate([value, value], axis), (n - by) % n, n, axis)


def per_device(tokens, gate_weight, pseudo_grad, anchor, momentum):
    zh, c = lax.axis_index("zh"), lax.axis_index("c")
    z, x, y = lax.axis_index("z"), lax.axis_index("x"), lax.axis_index("y")

    grad = pseudo_grad.reshape(2, 2, 1024, 128)
    got = flip(pick(grad, 1, 1 - c), "c")
    pair = pick(grad, 1, c).astype(F32) + got.astype(F32)
    mine, other = pick(pair, 0, zh), pick(pair, 0, 1 - zh)
    base = anchor - 0.567 * momentum
    half_done = (base - 0.3325 * mine).astype(BF)
    new_anchor, new_momentum, up_mine, up_other = [], [], [], []
    ups = []
    for part in range(2):
        rows = slice(512 * part, 512 * part + 512)
        out = jnp.stack([half_done[rows], other[rows].astype(BF)])
        back = flip(out, "zh").astype(F32)
        mean_delta = (mine[rows] + back[1]) / 4
        moved = 0.9 * momentum[rows] + mean_delta
        moved_anchor = anchor[rows] - 0.7 * (mean_delta + 0.9 * moved)
        new_momentum.append(moved)
        new_anchor.append(moved_anchor)
        a = moved_anchor.astype(BF)
        b = (back[0] - 0.3325 * other[rows]).astype(BF)
        ups.append(jnp.where(zh == 0, jnp.stack([a, b]), jnp.stack([b, a])))

    tok = tokens[0].reshape(8, 2, 2, 1024)
    own, away = pick(tok, 2, c), flip(pick(tok, 2, 1 - c), "c")
    tok = jnp.where(c == 0, jnp.stack([own, away]), jnp.stack([away, own]))
    tok = tok.reshape(16, 2048)
    beside = send(tok, lambda i: i ^ 1, "z")
    two = jnp.where(z % 2 == 0, jnp.stack([tok, beside]), jnp.stack([beside, tok]))
    three = jnp.stack([two, shift(two, "z", -2), shift(two, "z", 2)])
    six = roll_to(three, 0, z // 2).reshape(96, 2048)
    f1, b1 = shift(six, "y", 1), shift(six, "y", -1)
    f2, b2 = shift(f1, "y", 1), shift(b1, "y", -1)
    f3, b3 = shift(f2, "y", 1), shift(b2, "y", -1)
    f4, b4 = shift(f3[:48], "y", 1), shift(b3[48:], "y", -1)
    rows = jnp.concatenate([six, b1, b2, b3, f4, b4, f3, f2, f1])

    gate_own = pick(gate_weight.reshape(2, 2, 1024, 128), 1, c).reshape(2048, 128)
    gate_all = jnp.concatenate([gate_own] + [shift(gate_own, "x", -j) for j in (1, 2, 3)], axis=1)
    gate = jnp.dot(rows, gate_all, preferred_element_type=F32)

    up = 0.0
    for part in range(2):
        own = ups[part].reshape(1024, 128)
        columns = jnp.concatenate([own] + [shift(own, "x", -j) for j in (1, 2, 3)], axis=1)
        at = rows.reshape(768, 2, 1024)[:, :, 512 * part : 512 * part + 512].reshape(768, 1024)
        up = up + jnp.dot(at, columns, preferred_element_type=F32)

    def whole(partial):
        parts = partial.reshape(48, 2, 8, 512)
        got = flip(pick(parts, 1, 1 - c).astype(BF), "c")
        return pick(parts, 1, c) + got.astype(F32)

    hidden = (jax.nn.silu(whole(gate)) * whole(up)).astype(BF).reshape(384, 512)
    blocks = [hidden[:, 128 * j : 128 * j + 128] for j in range(4)]
    blocks = [blocks[0]] + [shift(blocks[j], "x", j) for j in (1, 2, 3)]
    result = jnp.stack([blocks[0], blocks[3], blocks[2], blocks[1]]).reshape(4, 8, 6, 8, 128)
    result = roll_to(roll_to(result, 0, x), 1, y)
    result = jnp.transpose(result, (2, 0, 1, 3, 4)).reshape(1, 1536, 128)
    return jnp.concatenate(new_anchor), jnp.concatenate(new_momentum), result


def solution(mesh):
    fine = Mesh(mesh.devices.reshape(ZH, C, Z, X, Y), AXES)
    rep, fsdp = ("zh", "c"), ("z", "x", "y")
    return jax.shard_map(
        lambda t, g, p, a, m: per_device(t, g, p[0], a, m),
        mesh=fine,
        in_specs=(P(rep, fsdp, None), P(None, fsdp), P(rep, None, fsdp), P(rep, fsdp), P(rep, fsdp)),
        out_specs=(P(rep, fsdp), P(rep, fsdp), P(rep, None, fsdp)),
        check_vma=False,
    )
```

```python
import functools

import jax
import jax.numpy as jnp
from jax import lax
from jax.experimental import pallas as pl
from jax.experimental.pallas import tpu as pltpu
from jax.sharding import Mesh, PartitionSpec as P

SIZES = {"zh": 2, "c": 2, "z": 6, "x": 4, "y": 8}
AXES = tuple(SIZES)
BF, F32 = jnp.bfloat16, jnp.float32
MIB = 1024 * 1024


def shift(value, axis, by):
    n = SIZES[axis]
    return lax.ppermute(value, axis, [(i, (i + by) % n) for i in range(n)])


def flip(value, axis):
    return lax.ppermute(value, axis, [(0, 1), (1, 0)])


def after(value, *others):
    return lax.optimization_barrier((value, *others))[0]


def whole(a):
    return pl.BlockSpec(a.shape, lambda i, at: (0,) * len(a.shape))


def call(body, scalars, arrays, outs, room=60):
    return pl.pallas_call(
        body,
        out_shape=outs,
        grid_spec=pltpu.PrefetchScalarGridSpec(
            num_scalar_prefetch=1,
            grid=(1,),
            in_specs=[whole(a) for a in arrays],
            out_specs=[whole(o) for o in outs],
        ),
        compiler_params=pltpu.CompilerParams(vmem_limit_bytes=room * MIB),
        cost_estimate=pl.CostEstimate(flops=0, bytes_accessed=1024, transcendentals=0),
    )(jnp.stack(scalars).astype(jnp.int32), *arrays)


def like(shape, dtype):
    return jax.ShapeDtypeStruct(shape, dtype)


def prepare_body(at, grad, got, anchor, momentum, out, half_done, mine, other):
    zh, c = at[0], at[1]
    s = grad[zh, c].astype(F32) + got[zh].astype(F32)
    o = grad[1 - zh, c].astype(F32) + got[1 - zh].astype(F32)
    v = (anchor[...] - 0.567 * momentum[...]) - 0.3325 * s
    mine[...] = s
    other[...] = o
    half_done[...] = v
    out[0] = v.astype(BF)
    out[1] = o.astype(BF)


def update_body(at, back, half_done, other, up):
    zh = at[0]
    up[zh] = (half_done[...] - 0.3325 * back[1].astype(F32)).astype(BF)
    up[1 - zh] = (back[0].astype(F32) - 0.3325 * other[...]).astype(BF)


def outer_body(at, mine, back, anchor, momentum, new_anchor, new_momentum):
    mean_delta = (mine[...] + back[1].astype(F32)) * 0.25
    moved = 0.9 * momentum[...] + mean_delta
    new_momentum[...] = moved
    new_anchor[...] = anchor[...] - 0.7 * (mean_delta + 0.9 * moved)


def product_body(at, *refs):
    tokens, weights, keep, give = refs[:9], refs[9:13], refs[13], refs[14]
    c, y = at[0], at[1]
    for half in range(2):
        pieces = tokens[:4] if half == 0 else tokens[4:]
        for pair in range(2):
            rows = jnp.concatenate([p[...] for p in pieces], axis=0)
            block = jnp.concatenate([w[...] for w in weights[2 * pair : 2 * pair + 2]], axis=1)
            total = jnp.dot(rows, block, preferred_element_type=F32)
            columns = slice(256 * pair, 256 * pair + 256)
            for s in range(4):
                low, high = total[96 * s : 96 * s + 48], total[96 * s + 48 : 96 * s + 96]
                place = lax.rem(y + 4 * half + s, 8)
                keep[place, :, columns] = jnp.where(c == 0, low, high)
                give[place, :, columns] = jnp.where(c == 0, high, low).astype(BF)


def product(c, y, tokens, weights):
    return call(product_body, [c, y], [*tokens, *weights], [like((8, 48, 512), F32), like((8, 48, 512), BF)])


def gated_body(at, gate, gate_got, up, up_got, hidden):
    x = at[0]
    for j in range(4):
        columns = slice(128 * j, 128 * j + 128)
        g = gate[:, :, columns] + gate_got[:, :, columns].astype(F32)
        u = up[:, :, columns] + up_got[:, :, columns].astype(F32)
        hidden[lax.rem(x + j, 4)] = (g / (1.0 + jnp.exp(-g)) * u).astype(BF)


def per_device(tokens, gate_weight, pseudo_grad, anchor, momentum):
    zh, c = lax.axis_index("zh"), lax.axis_index("c")
    x, y = lax.axis_index("x"), lax.axis_index("y")

    grad = pseudo_grad.reshape(2, 2, 1024, 128)
    pick = lax.dynamic_index_in_dim(grad, 1 - c, 1, keepdims=False)
    got = flip(pick, "c")
    tokens = after(tokens, pick)
    cut = jnp.transpose(tokens[0].reshape(8, 2, 2, 1024), (2, 0, 1, 3)).reshape(2, 1, 8, 2048)
    cut = jnp.broadcast_to(cut, (2, 6, 8, 2048)).reshape(12, 8, 2048)
    six = lax.all_to_all(cut, ("c", "z"), 0, 0).reshape(96, 2048)
    out, half_done, mine, other = call(
        prepare_body,
        [zh, c],
        [grad, got, anchor, momentum],
        [like((2, 1024, 128), BF)] + [like((1024, 128), F32)] * 3,
    )
    back = flip(out, "zh")
    six = after(six, out)
    f1, b1 = shift(six, "y", 1), shift(six, "y", -1)
    f2, b2 = shift(f1, "y", 1), shift(b1, "y", -1)
    (up,) = call(update_body, [zh], [back, half_done, other], [like((2, 1024, 128), BF)])
    ups = [up.reshape(2048, 128)]
    ups += [shift(ups[0], "x", -j) for j in (1, 2, 3)]
    f2, b2 = after(f2, up), after(b2, up)
    f3, b3 = shift(f2, "y", 1), shift(b2, "y", -1)
    own = lax.dynamic_index_in_dim(gate_weight.reshape(2, 2, 1024, 128), c, 1, keepdims=False).reshape(2048, 128)
    gate_blocks = [own] + [shift(own, "x", -j) for j in (1, 2, 3)]
    f3, b3, *gate_blocks = lax.optimization_barrier((f3, b3, *gate_blocks))
    f4, b4 = shift(f3[:48], "y", 1), shift(b3[48:], "y", -1)
    pieces = [six, b1, b2, b3, f4, b4, f3, f2, f1]

    gate, gate_give = product(c, y, pieces, gate_blocks)
    gate_got = flip(gate_give, "c")
    up, up_give = product(c, y, pieces, ups)
    up_got = flip(up_give, "c")

    (hidden,) = call(gated_body, [x], [gate, gate_got, up, up_got], [like((4, 8, 48, 128), BF)])
    hidden = lax.all_to_all(hidden, "x", 0, 0)
    hidden = jnp.transpose(hidden.reshape(4, 8, 6, 8, 128), (2, 0, 1, 3, 4)).reshape(1, 1536, 128)
    new_anchor, new_momentum = call(
        outer_body, [zh], [mine, back, anchor, momentum], [like((1024, 128), F32)] * 2
    )
    return new_anchor, new_momentum, hidden


def solution(mesh):
    fine = Mesh(mesh.devices.reshape(tuple(SIZES.values())), AXES)
    rep, fsdp = ("zh", "c"), ("z", "x", "y")
    return jax.shard_map(
        lambda t, g, p, a, m: per_device(t, g, p[0], a, m),
        mesh=fine,
        in_specs=(P(rep, fsdp, None), P(None, fsdp), P(rep, None, fsdp), P(rep, fsdp), P(rep, fsdp)),
        out_specs=(P(rep, fsdp), P(rep, fsdp), P(rep, None, fsdp)),
        check_vma=False,
    )
```

```python
import functools

import jax
import jax.numpy as jnp
from jax import lax
from jax.experimental import pallas as pl
from jax.experimental.pallas import tpu as pltpu
from jax.sharding import Mesh, PartitionSpec as P

SIZES = {"zh": 2, "c": 2, "z": 6, "x": 4, "y": 8}
AXES = tuple(SIZES)
BF, F32 = jnp.bfloat16, jnp.float32
MIB = 1024 * 1024
PARTS = 2
ROWS = 1024 // PARTS


def shift(value, axis, by):
    n = SIZES[axis]
    return lax.ppermute(value, axis, [(i, (i + by) % n) for i in range(n)])


def flip(value, axis):
    return lax.ppermute(value, axis, [(0, 1), (1, 0)])


def after(value, *others):
    return lax.optimization_barrier((value, *others))[0]


def whole(a):
    return pl.BlockSpec(a.shape, lambda i: (0,) * len(a.shape))


def like(shape, dtype):
    return jax.ShapeDtypeStruct(shape, dtype)


def call(body, arrays, outs, held=False, scratch=()):
    return pl.pallas_call(
        body,
        out_shape=outs,
        grid=(1,),
        in_specs=[pl.BlockSpec(memory_space=pl.ANY) if held else whole(a) for a in arrays],
        out_specs=[whole(o) for o in outs],
        scratch_shapes=list(scratch),
        compiler_params=pltpu.CompilerParams(vmem_limit_bytes=60 * MIB),
        cost_estimate=pl.CostEstimate(flops=0, bytes_accessed=1024, transcendentals=0),
    )(*arrays)


def prepare_body(grad, got, anchor, momentum, *outs):
    parts, (half_done, mine, other) = outs[:PARTS], outs[PARTS:]
    zh, c = lax.axis_index("zh"), lax.axis_index("c")
    s = grad[zh, c].astype(F32) + got[zh].astype(F32)
    o = grad[1 - zh, c].astype(F32) + got[1 - zh].astype(F32)
    v = (anchor[...] - 0.567 * momentum[...]) - 0.3325 * s
    mine[...] = s
    other[...] = o
    half_done[...] = v
    for part, ref in enumerate(parts):
        rows = slice(ROWS * part, ROWS * part + ROWS)
        ref[0] = v[rows].astype(BF)
        ref[1] = o[rows].astype(BF)


def update_body(part, back, half_done, other, up):
    zh = lax.axis_index("zh")
    rows = pl.ds(ROWS * part, ROWS)
    here = (half_done[rows] - 0.3325 * back[1].astype(F32)).astype(BF)
    there = (back[0].astype(F32) - 0.3325 * other[rows]).astype(BF)
    for x in range(4):
        up[x, zh] = here
        up[x, 1 - zh] = there


def outer_body(*refs):
    backs, (mine, anchor, momentum, new_anchor, new_momentum) = refs[:PARTS], refs[PARTS:]
    for part, ref in enumerate(backs):
        rows = pl.ds(ROWS * part, ROWS)
        mean_delta = (mine[rows] + ref[1].astype(F32)) * 0.25
        moved = 0.9 * momentum[rows] + mean_delta
        new_momentum[rows] = moved
        new_anchor[rows] = anchor[rows] - 0.7 * (mean_delta + 0.9 * moved)


def product_body(spans, *refs):
    tokens, weights = refs[:9], refs[9 : 9 + len(spans)]
    keep, give, rows, columns, sems = refs[9 + len(spans) :]
    c, y = lax.axis_index("c"), lax.axis_index("y")
    weight_copies, token_copies = [], []
    for pair in range(2):
        for x in (2 * pair, 2 * pair + 1):
            for source, runs in zip(weights, spans):
                for at, row, length in runs:
                    target = columns.at[pl.ds(at, length), pl.ds(128 * x, 128)]
                    weight_copies.append((pair, source.at[x, pl.ds(row, length)], target))
    for s, (piece, offset, length) in enumerate(
        [(t, 96 * s, 96) for s, t in enumerate(tokens[:4])]
        + [(tokens[4], 384, 48), (tokens[5], 432, 48)]
        + [(t, 96 * s, 96) for s, t in zip((5, 6, 7), tokens[6:])]
    ):
        place = lax.rem(y + offset // 96, 8) * 96 + offset % 96
        token_copies.append((0, piece, rows.at[pl.ds(pl.multiple_of(place, 16), length)]))
    order = [w for w in weight_copies if w[0] == 0] + token_copies + [w for w in weight_copies if w[0] == 1]
    copies = []
    for i, (pair, source, target) in enumerate(order):
        copy = pltpu.make_async_copy(source, target, sems.at[i])
        copy.start()
        copies.append((pair, copy))
    for pair in range(2):
        for at, copy in copies:
            if at == pair:
                copy.wait()
        span = slice(256 * pair, 256 * pair + 256)
        for half in range(2):
            total = jnp.dot(rows[384 * half : 384 * half + 384], columns[:, span], preferred_element_type=F32)
            for s in range(4):
                low, high = total[96 * s : 96 * s + 48], total[96 * s + 48 : 96 * s + 96]
                keep[4 * half + s, :, span] = jnp.where(c == 0, low, high)
                give[4 * half + s, :, span] = jnp.where(c == 0, high, low).astype(BF)


def product(spans, tokens, weights):
    count = 9 + 4 * sum(len(s) for s in spans)
    return call(
        functools.partial(product_body, spans),
        [*tokens, *weights],
        [like((8, 48, 512), F32), like((8, 48, 512), BF)],
        True,
        [pltpu.VMEM((768, 2048), BF), pltpu.VMEM((2048, 512), BF), pltpu.SemaphoreType.DMA((count,))],
    )


def gated_body(gate, gate_got, up, up_got, hidden):
    for x in range(4):
        columns = slice(128 * x, 128 * x + 128)
        g = gate[:, :, columns] + gate_got[:, :, columns].astype(F32)
        u = up[:, :, columns] + up_got[:, :, columns].astype(F32)
        hidden[x] = (g / (1.0 + jnp.exp(-g)) * u).astype(BF)


def per_device(tokens, gate_weight, pseudo_grad, anchor, momentum):
    c = lax.axis_index("c")

    grad = pseudo_grad.reshape(2, 2, 1024, 128)
    pick = lax.dynamic_index_in_dim(grad, 1 - c, 1, keepdims=False)
    got = flip(pick, "c")
    *parts, half_done, mine, other = call(
        prepare_body,
        [grad, got, anchor, momentum],
        [like((2, ROWS, 128), BF)] * PARTS + [like((1024, 128), F32)] * 3,
    )
    tokens = after(tokens, pick)
    cut = jnp.transpose(tokens[0].reshape(8, 2, 2, 1024), (2, 0, 1, 3)).reshape(2, 1, 8, 2048)
    cut = jnp.broadcast_to(cut, (2, 6, 8, 2048)).reshape(12, 8, 2048)
    six = lax.all_to_all(cut, ("c", "z"), 0, 0).reshape(96, 2048)
    six = after(six, parts[0])
    own = lax.dynamic_index_in_dim(gate_weight.reshape(2, 2, 1024, 128), c, 1, keepdims=False).reshape(1, 2048, 128)
    own = after(jnp.broadcast_to(own, (4, 2048, 128)), six)

    def update(part):
        (up,) = call(functools.partial(update_body, part), [backs[part], half_done, other], [like((4, 2, ROWS, 128), BF)])
        return up.reshape(4, 2 * ROWS, 128)

    first = [shift(six, "y", by) for by in (2, -2, 1, -1)] + [flip(parts[0], "zh")]
    f2, b2, f1, b1, back, gate_all = lax.optimization_barrier((*first, lax.all_to_all(own, "x", 0, 0)))
    backs = [back]
    second = [shift(f1, "y", 2), shift(b1, "y", -2), shift(f2[:48], "y", 2), shift(b2[48:], "y", -2), flip(parts[1], "zh")]
    f3, b3, f4, b4, back, up = lax.optimization_barrier((*second, lax.all_to_all(update(0), "x", 0, 0)))
    backs.append(back)
    ups = [up, lax.all_to_all(update(1), "x", 0, 0)]
    pieces = [six, b1, b2, b3, f4, b4, f3, f2, f1]
    gate, gate_give = product((((0, 0, 2048),),), pieces, [gate_all])
    gate_got = flip(gate_give, "c")
    spans = tuple(((ROWS * p, 0, ROWS), (1024 + ROWS * p, ROWS, ROWS)) for p in range(PARTS))
    up, up_give = product(spans, pieces, ups)
    up_got = flip(up_give, "c")

    (hidden,) = call(gated_body, [gate, gate_got, up, up_got], [like((4, 8, 48, 128), BF)])
    hidden = lax.all_to_all(hidden, "x", 0, 0)
    hidden = jnp.transpose(hidden.reshape(4, 8, 6, 8, 128), (2, 0, 1, 3, 4)).reshape(1, 1536, 128)
    new_anchor, new_momentum = call(outer_body, [*backs, mine, anchor, momentum], [like((1024, 128), F32)] * 2)
    return new_anchor, new_momentum, hidden


def solution(mesh):
    fine = Mesh(mesh.devices.reshape(tuple(SIZES.values())), AXES)
    rep, fsdp = ("zh", "c"), ("z", "x", "y")
    return jax.shard_map(
        lambda t, g, p, a, m: per_device(t, g, p[0], a, m),
        mesh=fine,
        in_specs=(P(rep, fsdp, None), P(None, fsdp), P(rep, None, fsdp), P(rep, fsdp), P(rep, fsdp)),
        out_specs=(P(rep, fsdp), P(rep, fsdp), P(rep, None, fsdp)),
        check_vma=False,
    )
```

```python
import functools

import jax
import jax.numpy as jnp
from jax import lax
from jax.experimental import pallas as pl
from jax.experimental.pallas import tpu as pltpu
from jax.sharding import Mesh, PartitionSpec as P

SIZES = {"zh": 2, "c": 2, "z": 6, "x": 4, "y": 8}
AXES = tuple(SIZES)
BF, F32 = jnp.bfloat16, jnp.float32
MIB = 1024 * 1024
PARTS = 1
ROWS = 1024 // PARTS


def shift(value, axis, by):
    n = SIZES[axis]
    return lax.ppermute(value, axis, [(i, (i + by) % n) for i in range(n)])


def flip(value, axis):
    return lax.ppermute(value, axis, [(0, 1), (1, 0)])


def along(value):
    pairs = []
    for zh in range(2):
        for c in range(2):
            for z in range(6):
                to = (6 * zh + z + (3 if c == 0 else -3)) % 12
                pairs.append(((2 * zh + c) * 6 + z, (2 * (to // 6) + c) * 6 + to % 6))
    return lax.ppermute(value, ("zh", "c", "z"), pairs)


def after(value, *others):
    return lax.optimization_barrier((value, *others))[0]


def whole(a):
    return pl.BlockSpec(a.shape, lambda i: (0,) * len(a.shape))


def like(shape, dtype):
    return jax.ShapeDtypeStruct(shape, dtype)


def call(body, arrays, outs, held=False, scratch=()):
    return pl.pallas_call(
        body,
        out_shape=outs,
        grid=(1,),
        in_specs=[pl.BlockSpec(memory_space=pl.ANY) if held else whole(a) for a in arrays],
        out_specs=[whole(o) for o in outs],
        scratch_shapes=list(scratch),
        compiler_params=pltpu.CompilerParams(vmem_limit_bytes=60 * MIB),
        cost_estimate=pl.CostEstimate(flops=0, bytes_accessed=1024, transcendentals=0),
    )(*arrays)


def prepare_body(grad, got, anchor, momentum, *outs):
    parts, (half_done, mine, other) = outs[:PARTS], outs[PARTS:]
    zh, c = lax.axis_index("zh"), lax.axis_index("c")
    s = grad[zh, c].astype(F32) + got[zh].astype(F32)
    o = grad[1 - zh, c].astype(F32) + got[1 - zh].astype(F32)
    v = (anchor[...] - 0.567 * momentum[...]) - 0.3325 * s
    mine[...] = s
    other[...] = o
    half_done[...] = v
    for part, ref in enumerate(parts):
        rows = slice(ROWS * part, ROWS * part + ROWS)
        ref[0] = v[rows].astype(BF)
        ref[1] = o[rows].astype(BF)


def update_body(part, back, half_done, other, up):
    zh = lax.axis_index("zh")
    rows = pl.ds(ROWS * part, ROWS)
    here = (half_done[rows] - 0.3325 * back[1].astype(F32)).astype(BF)
    there = (back[0].astype(F32) - 0.3325 * other[rows]).astype(BF)
    for x in range(4):
        up[x, zh] = here
        up[x, 1 - zh] = there


def outer_body(*refs):
    backs, (mine, anchor, momentum, new_anchor, new_momentum) = refs[:PARTS], refs[PARTS:]
    for part, ref in enumerate(backs):
        rows = pl.ds(ROWS * part, ROWS)
        mean_delta = (mine[rows] + ref[1].astype(F32)) * 0.25
        moved = 0.9 * momentum[rows] + mean_delta
        new_momentum[rows] = moved
        new_anchor[rows] = anchor[rows] - 0.7 * (mean_delta + 0.9 * moved)


def product_body(spans, *refs):
    tokens, weights = refs[:9], refs[9 : 9 + len(spans)]
    keep, give, rows, columns, sems = refs[9 + len(spans) :]
    c, y = lax.axis_index("c"), lax.axis_index("y")
    weight_copies, token_copies = ([], []), ([], [])
    for x in range(4):
        for source, runs in zip(weights, spans):
            for at, row, length in runs:
                target = columns.at[pl.ds(at, length), pl.ds(128 * x, 128)]
                weight_copies[x // 2].append((source.at[x, pl.ds(row, length)], target))
    for piece, at, length in zip(tokens, (0, 96, 192, 288, 384, 432, 480, 576, 672), (96, 96, 96, 96, 48, 48, 96, 96, 96)):
        token_copies[at // 384].append((piece, rows.at[pl.ds(at, length)]))
    count, stages = 0, []
    for stage in (weight_copies[0] + token_copies[0], token_copies[1], weight_copies[1]):
        copies = []
        for source, target in stage:
            copy = pltpu.make_async_copy(source, target, sems.at[count])
            copy.start()
            copies.append(copy)
            count += 1
        stages.append(copies)
    for pair in range(2):
        span = slice(256 * pair, 256 * pair + 256)
        for half in range(2):
            for copy in stages[2 * pair + half] if pair + half < 2 or half == 0 else ():
                copy.wait()
            total = jnp.dot(rows[384 * half : 384 * half + 384], columns[:, span], preferred_element_type=F32)
            for s in range(4):
                low, high = total[96 * s : 96 * s + 48], total[96 * s + 48 : 96 * s + 96]
                place = lax.rem(y + 4 * half + s, 8)
                keep[place, :, span] = jnp.where(c == 0, low, high)
                give[place, :, span] = jnp.where(c == 0, high, low).astype(BF)


def product(spans, tokens, weights):
    count = 9 + 4 * sum(len(s) for s in spans)
    return call(
        functools.partial(product_body, spans),
        [*tokens, *weights],
        [like((8, 48, 512), F32), like((8, 48, 512), BF)],
        True,
        [pltpu.VMEM((768, 2048), BF), pltpu.VMEM((2048, 512), BF), pltpu.SemaphoreType.DMA((count,))],
    )


def gated_body(gate, gate_got, up, up_got, hidden):
    for x in range(4):
        columns = slice(128 * x, 128 * x + 128)
        g = gate[:, :, columns] + gate_got[:, :, columns].astype(F32)
        u = up[:, :, columns] + up_got[:, :, columns].astype(F32)
        hidden[x] = (g / (1.0 + jnp.exp(-g)) * u).astype(BF)


def per_device(tokens, gate_weight, pseudo_grad, anchor, momentum):
    c = lax.axis_index("c")

    grad = pseudo_grad.reshape(2, 2, 1024, 128)
    pick = lax.dynamic_index_in_dim(grad, 1 - c, 1, keepdims=False)
    got = flip(pick, "c")
    *parts, half_done, mine, other = call(
        prepare_body,
        [grad, got, anchor, momentum],
        [like((2, ROWS, 128), BF)] * PARTS + [like((1024, 128), F32)] * 3,
    )
    tokens = after(tokens, pick)
    cut = jnp.transpose(tokens[0].reshape(8, 2, 2, 1024), (2, 0, 1, 3)).reshape(2, 1, 8, 2048)
    cut = jnp.broadcast_to(cut, (2, 6, 8, 2048)).reshape(12, 8, 2048)
    six = lax.all_to_all(cut, ("c", "z"), 0, 0).reshape(96, 2048)
    six = after(six, parts[0])
    own = lax.dynamic_index_in_dim(gate_weight.reshape(2, 2, 1024, 128), c, 1, keepdims=False).reshape(1, 2048, 128)
    own = after(jnp.broadcast_to(own, (4, 2048, 128)), six)

    def update(part):
        (up,) = call(functools.partial(update_body, part), [backs[part], half_done, other], [like((4, 2, ROWS, 128), BF)])
        return up.reshape(4, 2 * ROWS, 128)

    gate_all = lax.all_to_all(own, "x", 0, 0)
    f1, b1 = shift(six, "y", 1), shift(six, "y", -1)
    f1, b1, back = lax.optimization_barrier((f1, b1, along(parts[0])))
    f2, b2 = shift(f1, "y", 1), shift(b1, "y", -1)
    f2, b2, back, gate_all = lax.optimization_barrier((f2, b2, along(back), gate_all))
    backs = [back]
    f3, b3 = shift(f2, "y", 1), shift(b2, "y", -1)
    f4, b4 = shift(f3[:48], "y", 1), shift(b3[48:], "y", -1)
    pieces = [six, b1, b2, b3, f4, b4, f3, f2, f1]
    ups = [lax.all_to_all(update(0), "x", 0, 0)]
    gate, gate_give = product((((0, 0, 2048),),), pieces, [gate_all])
    gate_got = flip(gate_give, "c")
    spans = tuple(((ROWS * p, 0, ROWS), (1024 + ROWS * p, ROWS, ROWS)) for p in range(PARTS))
    up, up_give = product(spans, pieces, ups)
    up_got = flip(up_give, "c")

    (hidden,) = call(gated_body, [gate, gate_got, up, up_got], [like((4, 8, 48, 128), BF)])
    hidden = lax.all_to_all(hidden, "x", 0, 0)
    hidden = jnp.transpose(hidden.reshape(4, 8, 6, 8, 128), (2, 0, 1, 3, 4)).reshape(1, 1536, 128)
    new_anchor, new_momentum = call(outer_body, [*backs, mine, anchor, momentum], [like((1024, 128), F32)] * 2)
    return new_anchor, new_momentum, hidden


def solution(mesh):
    fine = Mesh(mesh.devices.reshape(tuple(SIZES.values())), AXES)
    rep, fsdp = ("zh", "c"), ("z", "x", "y")
    return jax.shard_map(
        lambda t, g, p, a, m: per_device(t, g, p[0], a, m),
        mesh=fine,
        in_specs=(P(rep, fsdp, None), P(None, fsdp), P(rep, None, fsdp), P(rep, fsdp), P(rep, fsdp)),
        out_specs=(P(rep, fsdp), P(rep, fsdp), P(rep, None, fsdp)),
        check_vma=False,
    )
```

```python
import functools

import jax
import jax.numpy as jnp
from jax import lax
from jax.experimental import pallas as pl
from jax.experimental.pallas import tpu as pltpu
from jax.sharding import Mesh, PartitionSpec as P

SIZES = {"zh": 2, "c": 2, "z": 6, "x": 4, "y": 8}
AXES = tuple(SIZES)
BF, F32 = jnp.bfloat16, jnp.float32
MIB = 1024 * 1024
PARTS = 1
ROWS = 1024 // PARTS


def shift(value, axis, by):
    n = SIZES[axis]
    return lax.ppermute(value, axis, [(i, (i + by) % n) for i in range(n)])


def flip(value, axis):
    return lax.ppermute(value, axis, [(0, 1), (1, 0)])


def along(value, hops):
    pairs = []
    for zh in range(2):
        for c in range(2):
            for z in range(6):
                to = (6 * zh + z + (hops if c == 0 else -hops)) % 12
                pairs.append(((2 * zh + c) * 6 + z, (2 * (to // 6) + c) * 6 + to % 6))
    return lax.ppermute(value, ("zh", "c", "z"), pairs)


def after(value, *others):
    return lax.optimization_barrier((value, *others))[0]


def whole(a):
    return pl.BlockSpec(a.shape, lambda i: (0,) * len(a.shape))


def like(shape, dtype):
    return jax.ShapeDtypeStruct(shape, dtype)


def call(body, arrays, outs, held=False, scratch=()):
    return pl.pallas_call(
        body,
        out_shape=outs,
        grid=(1,),
        in_specs=[pl.BlockSpec(memory_space=pl.ANY) if held else whole(a) for a in arrays],
        out_specs=[whole(o) for o in outs],
        scratch_shapes=list(scratch),
        compiler_params=pltpu.CompilerParams(vmem_limit_bytes=60 * MIB),
        cost_estimate=pl.CostEstimate(flops=0, bytes_accessed=1024, transcendentals=0),
    )(*arrays)


def prepare_body(grad, got, anchor, momentum, *outs):
    parts, (half_done, mine, other) = outs[:PARTS], outs[PARTS:]
    zh, c = lax.axis_index("zh"), lax.axis_index("c")
    s = grad[zh, c].astype(F32) + got[zh].astype(F32)
    o = grad[1 - zh, c].astype(F32) + got[1 - zh].astype(F32)
    v = (anchor[...] - 0.567 * momentum[...]) - 0.3325 * s
    mine[...] = s
    other[...] = o
    half_done[...] = v
    for part, ref in enumerate(parts):
        rows = slice(ROWS * part, ROWS * part + ROWS)
        ref[0] = v[rows].astype(BF)
        ref[1] = o[rows].astype(BF)


def update_body(part, back, half_done, other, up):
    zh = lax.axis_index("zh")
    rows = pl.ds(ROWS * part, ROWS)
    here = (half_done[rows] - 0.3325 * back[1].astype(F32)).astype(BF)
    there = (back[0].astype(F32) - 0.3325 * other[rows]).astype(BF)
    for x in range(4):
        up[x, zh] = here
        up[x, 1 - zh] = there


def outer_body(*refs):
    backs, (mine, anchor, momentum, new_anchor, new_momentum) = refs[:PARTS], refs[PARTS:]
    for part, ref in enumerate(backs):
        rows = pl.ds(ROWS * part, ROWS)
        mean_delta = (mine[rows] + ref[1].astype(F32)) * 0.25
        moved = 0.9 * momentum[rows] + mean_delta
        new_momentum[rows] = moved
        new_anchor[rows] = anchor[rows] - 0.7 * (mean_delta + 0.9 * moved)


def product_body(*refs):
    tokens, weights = refs[:9], refs[9:-5]
    keep, give, rows, columns, sems = refs[-5:]
    c, x, y = lax.axis_index("c"), lax.axis_index("x"), lax.axis_index("y")
    copies = []
    if len(weights) == 4:
        for j, source in enumerate(weights):
            copies.append((0, source, columns.at[:, pl.ds(pl.multiple_of(128 * lax.rem(x + j, 4), 128), 128)]))
    else:
        for j in range(4):
            copies.append((j // 2, weights[0].at[j], columns.at[:, pl.ds(128 * j, 128)]))
    for piece, at, length in zip(tokens, (0, 96, 192, 288, 384, 432, 480, 576, 672), (96, 96, 96, 96, 48, 48, 96, 96, 96)):
        place = lax.rem(y + at // 96, 8) * 96 + at % 96
        copies.append((0, piece, rows.at[pl.ds(pl.multiple_of(place, 16), length)]))
    copies.sort(key=lambda entry: entry[0])
    started = []
    for i, (stage, source, target) in enumerate(copies):
        copy = pltpu.make_async_copy(source, target, sems.at[i])
        copy.start()
        started.append((stage, copy))
    for pair in range(2):
        for stage, copy in started:
            if stage == pair:
                copy.wait()
        span = slice(256 * pair, 256 * pair + 256)
        for half in range(2):
            total = jnp.dot(rows[384 * half : 384 * half + 384], columns[:, span], preferred_element_type=F32)
            for s in range(4):
                low, high = total[96 * s : 96 * s + 48], total[96 * s + 48 : 96 * s + 96]
                keep[4 * half + s, :, span] = jnp.where(c == 0, low, high)
                give[4 * half + s, :, span] = jnp.where(c == 0, high, low).astype(BF)


def product(tokens, weights):
    return call(
        product_body,
        [*tokens, *weights],
        [like((8, 48, 512), F32), like((8, 48, 512), BF)],
        True,
        [pltpu.VMEM((768, 2048), BF), pltpu.VMEM((2048, 512), BF), pltpu.SemaphoreType.DMA((13,))],
    )


def gated_body(gate, gate_got, up, up_got, hidden):
    for x in range(4):
        columns = slice(128 * x, 128 * x + 128)
        g = gate[:, :, columns] + gate_got[:, :, columns].astype(F32)
        u = up[:, :, columns] + up_got[:, :, columns].astype(F32)
        hidden[x] = (g / (1.0 + jnp.exp(-g)) * u).astype(BF)


def per_device(tokens, gate_weight, pseudo_grad, anchor, momentum):
    c = lax.axis_index("c")

    grad = pseudo_grad.reshape(2, 2, 1024, 128)
    pick = lax.dynamic_index_in_dim(grad, 1 - c, 1, keepdims=False)
    got = flip(pick, "c")
    *parts, half_done, mine, other = call(
        prepare_body,
        [grad, got, anchor, momentum],
        [like((2, ROWS, 128), BF)] * PARTS + [like((1024, 128), F32)] * 3,
    )
    tokens = after(tokens, pick)
    cut = jnp.transpose(tokens[0].reshape(8, 2, 2, 1024), (2, 0, 1, 3)).reshape(2, 1, 8, 2048)
    cut = jnp.broadcast_to(cut, (2, 6, 8, 2048)).reshape(12, 8, 2048)
    six = lax.all_to_all(cut, ("c", "z"), 0, 0).reshape(96, 2048)
    own = lax.dynamic_index_in_dim(gate_weight.reshape(2, 2, 1024, 128), c, 1, keepdims=False).reshape(2048, 128)

    back = along(parts[0], 3)
    six, back = lax.optimization_barrier((six, back))
    first = (shift(six, "y", 1), shift(six, "y", -1), along(back, 3), shift(own, "x", -1), shift(own, "x", 1))
    f1, b1, back, g1, g3 = lax.optimization_barrier(first)
    (up,) = call(functools.partial(update_body, 0), [back, half_done, other], [like((4, 2, 1024, 128), BF)])
    up_all = lax.all_to_all(up.reshape(4, 2048, 128), "x", 0, 0)
    f2, b2, g2 = lax.optimization_barrier((shift(f1, "y", 1), shift(b1, "y", -1), shift(own, "x", 2)))
    f3, b3 = shift(f2, "y", 1), shift(b2, "y", -1)
    f4, b4 = shift(f2[:48], "y", 2), shift(b2[48:], "y", -2)
    pieces = [six, b1, b2, b3, f4, b4, f3, f2, f1]
    gate, gate_give = product(pieces, [own, g1, g2, g3])
    gate_got = flip(gate_give, "c")
    up, up_give = product(pieces, [up_all])
    up_got = flip(up_give, "c")

    (hidden,) = call(gated_body, [gate, gate_got, up, up_got], [like((4, 8, 48, 128), BF)])
    hidden = lax.all_to_all(hidden, "x", 0, 0)
    hidden = jnp.transpose(hidden.reshape(4, 8, 6, 8, 128), (2, 0, 1, 3, 4)).reshape(1, 1536, 128)
    new_anchor, new_momentum = call(outer_body, [back, mine, anchor, momentum], [like((1024, 128), F32)] * 2)
    return new_anchor, new_momentum, hidden


def solution(mesh):
    fine = Mesh(mesh.devices.reshape(tuple(SIZES.values())), AXES)
    rep, fsdp = ("zh", "c"), ("z", "x", "y")
    return jax.shard_map(
        lambda t, g, p, a, m: per_device(t, g, p[0], a, m),
        mesh=fine,
        in_specs=(P(rep, fsdp, None), P(None, fsdp), P(rep, None, fsdp), P(rep, fsdp), P(rep, fsdp)),
        out_specs=(P(rep, fsdp), P(rep, fsdp), P(rep, None, fsdp)),
        check_vma=False,
    )
```

```python
import functools

import jax
import jax.numpy as jnp
from jax import lax
from jax.experimental import pallas as pl
from jax.experimental.pallas import tpu as pltpu
from jax.sharding import Mesh, PartitionSpec as P

SIZES = {"zh": 2, "c": 2, "z": 6, "x": 4, "y": 8}
AXES = tuple(SIZES)
BF, F32 = jnp.bfloat16, jnp.float32
MIB = 1024 * 1024
PARTS = 1
ROWS = 1024 // PARTS


def shift(value, axis, by):
    n = SIZES[axis]
    return lax.ppermute(value, axis, [(i, (i + by) % n) for i in range(n)])


def flip(value, axis):
    return lax.ppermute(value, axis, [(0, 1), (1, 0)])


def along(value, hops):
    pairs = []
    for zh in range(2):
        for c in range(2):
            for z in range(6):
                to = (6 * zh + z + (hops if c == 0 else -hops)) % 12
                pairs.append(((2 * zh + c) * 6 + z, (2 * (to // 6) + c) * 6 + to % 6))
    return lax.ppermute(value, ("zh", "c", "z"), pairs)


def after(value, *others):
    return lax.optimization_barrier((value, *others))[0]


def whole(a):
    return pl.BlockSpec(a.shape, lambda i: (0,) * len(a.shape))


def like(shape, dtype):
    return jax.ShapeDtypeStruct(shape, dtype)


def call(body, arrays, outs, held=False, scratch=()):
    return pl.pallas_call(
        body,
        out_shape=outs,
        grid=(1,),
        in_specs=[pl.BlockSpec(memory_space=pl.ANY) if held else whole(a) for a in arrays],
        out_specs=[whole(o) for o in outs],
        scratch_shapes=list(scratch),
        compiler_params=pltpu.CompilerParams(vmem_limit_bytes=60 * MIB),
        cost_estimate=pl.CostEstimate(flops=0, bytes_accessed=1024, transcendentals=0),
    )(*arrays)


def prepare_body(grad, got, anchor, momentum, *outs):
    parts, (half_done, mine, other) = outs[:PARTS], outs[PARTS:]
    zh, c = lax.axis_index("zh"), lax.axis_index("c")
    s = grad[zh, c].astype(F32) + got[zh].astype(F32)
    o = grad[1 - zh, c].astype(F32) + got[1 - zh].astype(F32)
    v = (anchor[...] - 0.567 * momentum[...]) - 0.3325 * s
    mine[...] = s
    other[...] = o
    half_done[...] = v
    for part, ref in enumerate(parts):
        rows = slice(ROWS * part, ROWS * part + ROWS)
        ref[0] = v[rows].astype(BF)
        ref[1] = o[rows].astype(BF)


def update_body(part, back, half_done, other, up):
    zh = lax.axis_index("zh")
    rows = pl.ds(ROWS * part, ROWS)
    here = (half_done[rows] - 0.3325 * back[1].astype(F32)).astype(BF)
    there = (back[0].astype(F32) - 0.3325 * other[rows]).astype(BF)
    for x in range(4):
        up[x, zh] = here
        up[x, 1 - zh] = there


def outer_body(*refs):
    backs, (mine, anchor, momentum, new_anchor, new_momentum) = refs[:PARTS], refs[PARTS:]
    for part, ref in enumerate(backs):
        rows = pl.ds(ROWS * part, ROWS)
        mean_delta = (mine[rows] + ref[1].astype(F32)) * 0.25
        moved = 0.9 * momentum[rows] + mean_delta
        new_momentum[rows] = moved
        new_anchor[rows] = anchor[rows] - 0.7 * (mean_delta + 0.9 * moved)


def product_body(*refs):
    tokens, weights = refs[:9], refs[9:11]
    keep, give, rows, columns, sems = refs[11:]
    c, y = lax.axis_index("c"), lax.axis_index("y")
    sources = []
    for piece, at, length in zip(tokens, (0, 96, 192, 288, 384, 432, 480, 576, 672), (96, 96, 96, 96, 48, 48, 96, 96, 96)):
        place = lax.rem(y + at // 96, 8) * 96 + at % 96
        sources.append((0, piece, rows.at[pl.ds(pl.multiple_of(place, 16), length)]))
    for kind in range(2):
        for x in range(4):
            target = columns.at[kind, :, pl.ds(128 * x, 128)]
            sources.append((2 * kind + x // 2, weights[kind].at[x], target))
    copies = []
    for i, (stage, source, target) in enumerate(sources):
        copy = pltpu.make_async_copy(source, target, sems.at[i])
        copy.start()
        copies.append((stage, copy))
    for stage in range(4):
        for at, copy in copies:
            if at == stage:
                copy.wait()
        kind, pair = stage // 2, stage % 2
        span = slice(256 * pair, 256 * pair + 256)
        for half in range(2):
            total = jnp.dot(rows[384 * half : 384 * half + 384], columns[kind, :, span], preferred_element_type=F32)
            for s in range(4):
                low, high = total[96 * s : 96 * s + 48], total[96 * s + 48 : 96 * s + 96]
                keep[kind, 4 * half + s, :, span] = jnp.where(c == 0, low, high).astype(BF)
                give[kind, 4 * half + s, :, span] = jnp.where(c == 0, high, low).astype(BF)


def product(tokens, gate, up):
    return call(
        product_body,
        [*tokens, gate, up],
        [like((2, 8, 48, 512), BF)] * 2,
        True,
        [pltpu.VMEM((768, 2048), BF), pltpu.VMEM((2, 2048, 512), BF), pltpu.SemaphoreType.DMA((17,))],
    )


def gated_body(keep, got, hidden):
    for x in range(4):
        columns = slice(128 * x, 128 * x + 128)
        g = keep[0, :, :, columns].astype(F32) + got[0, :, :, columns].astype(F32)
        u = keep[1, :, :, columns].astype(F32) + got[1, :, :, columns].astype(F32)
        hidden[x] = (g / (1.0 + jnp.exp(-g)) * u).astype(BF)


def per_device(tokens, gate_weight, pseudo_grad, anchor, momentum):
    c = lax.axis_index("c")

    grad = pseudo_grad.reshape(2, 2, 1024, 128)
    pick = lax.dynamic_index_in_dim(grad, 1 - c, 1, keepdims=False)
    got = flip(pick, "c")
    *parts, half_done, mine, other = call(
        prepare_body,
        [grad, got, anchor, momentum],
        [like((2, ROWS, 128), BF)] * PARTS + [like((1024, 128), F32)] * 3,
    )
    tokens = after(tokens, pick)
    cut = jnp.transpose(tokens[0].reshape(8, 2, 2, 1024), (2, 0, 1, 3)).reshape(2, 1, 8, 2048)
    cut = jnp.broadcast_to(cut, (2, 6, 8, 2048)).reshape(12, 8, 2048)
    six = lax.all_to_all(cut, ("c", "z"), 0, 0).reshape(96, 2048)
    own = lax.dynamic_index_in_dim(gate_weight.reshape(2, 2, 1024, 128), c, 1, keepdims=False).reshape(1, 2048, 128)
    own = jnp.broadcast_to(own, (4, 2048, 128))

    back = along(parts[0], 1)
    six, back, own = lax.optimization_barrier((six, back, own))
    first = [along(back, 5)] + [shift(six, "y", by) for by in (2, -2, 1, -1)]
    back, f2, b2, f1, b1, gate_all = lax.optimization_barrier((*first, lax.all_to_all(own, "x", 0, 0)))
    (up,) = call(functools.partial(update_body, 0), [back, half_done, other], [like((4, 2, 1024, 128), BF)])
    up_all = lax.all_to_all(up.reshape(4, 2048, 128), "x", 0, 0)
    f3, b3 = shift(f1, "y", 2), shift(b1, "y", -2)
    f4, b4 = shift(f2[:48], "y", 2), shift(b2[48:], "y", -2)
    keep, give = product([six, b1, b2, b3, f4, b4, f3, f2, f1], gate_all, up_all)
    (hidden,) = call(gated_body, [keep, flip(give, "c")], [like((4, 8, 48, 128), BF)])
    hidden = lax.all_to_all(hidden, "x", 0, 0)
    hidden = jnp.transpose(hidden.reshape(4, 8, 6, 8, 128), (2, 0, 1, 3, 4)).reshape(1, 1536, 128)
    new_anchor, new_momentum = call(outer_body, [back, mine, anchor, momentum], [like((1024, 128), F32)] * 2)
    return new_anchor, new_momentum, hidden


def solution(mesh):
    fine = Mesh(mesh.devices.reshape(tuple(SIZES.values())), AXES)
    rep, fsdp = ("zh", "c"), ("z", "x", "y")
    return jax.shard_map(
        lambda t, g, p, a, m: per_device(t, g, p[0], a, m),
        mesh=fine,
        in_specs=(P(rep, fsdp, None), P(None, fsdp), P(rep, None, fsdp), P(rep, fsdp), P(rep, fsdp)),
        out_specs=(P(rep, fsdp), P(rep, fsdp), P(rep, None, fsdp)),
        check_vma=False,
    )
```

```python
import functools

import jax
import jax.numpy as jnp
from jax import lax
from jax.experimental import pallas as pl
from jax.experimental.pallas import tpu as pltpu
from jax.sharding import Mesh, PartitionSpec as P

SIZES = {"zh": 2, "c": 2, "z": 6, "x": 4, "y": 8}
AXES = tuple(SIZES)
BF, F32 = jnp.bfloat16, jnp.float32
MIB = 1024 * 1024
PARTS = 1
ROWS = 1024 // PARTS


def shift(value, axis, by):
    n = SIZES[axis]
    return lax.ppermute(value, axis, [(i, (i + by) % n) for i in range(n)])


def flip(value, axis):
    return lax.ppermute(value, axis, [(0, 1), (1, 0)])


def after(value, *others):
    return lax.optimization_barrier((value, *others))[0]


def whole(a):
    return pl.BlockSpec(a.shape, lambda i: (0,) * len(a.shape))


def like(shape, dtype):
    return jax.ShapeDtypeStruct(shape, dtype)


def call(body, arrays, outs, held=False, scratch=()):
    return pl.pallas_call(
        body,
        out_shape=outs,
        grid=(1,),
        in_specs=[pl.BlockSpec(memory_space=pl.ANY) if held else whole(a) for a in arrays],
        out_specs=[whole(o) for o in outs],
        scratch_shapes=list(scratch),
        compiler_params=pltpu.CompilerParams(vmem_limit_bytes=60 * MIB),
        cost_estimate=pl.CostEstimate(flops=0, bytes_accessed=1024, transcendentals=0),
    )(*arrays)


def prepare_body(grad, got, anchor, momentum, *outs):
    parts, (half_done, mine, other) = outs[:PARTS], outs[PARTS:]
    zh, c = lax.axis_index("zh"), lax.axis_index("c")
    s = grad[zh, c].astype(F32) + got[zh].astype(F32)
    o = grad[1 - zh, c].astype(F32) + got[1 - zh].astype(F32)
    v = (anchor[...] - 0.567 * momentum[...]) - 0.3325 * s
    mine[...] = s
    other[...] = o
    half_done[...] = v
    for part, ref in enumerate(parts):
        rows = slice(ROWS * part, ROWS * part + ROWS)
        ref[0] = v[rows].astype(BF)
        ref[1] = o[rows].astype(BF)


def update_body(part, back, half_done, other, up):
    zh = lax.axis_index("zh")
    rows = pl.ds(ROWS * part, ROWS)
    here = (half_done[rows] - 0.3325 * back[1].astype(F32)).astype(BF)
    there = (back[0].astype(F32) - 0.3325 * other[rows]).astype(BF)
    up[zh] = here
    up[1 - zh] = there


def outer_body(*refs):
    backs, (mine, anchor, momentum, new_anchor, new_momentum) = refs[:PARTS], refs[PARTS:]
    for part, ref in enumerate(backs):
        rows = pl.ds(ROWS * part, ROWS)
        mean_delta = (mine[rows] + ref[1].astype(F32)) * 0.25
        moved = 0.9 * momentum[rows] + mean_delta
        new_momentum[rows] = moved
        new_anchor[rows] = anchor[rows] - 0.7 * (mean_delta + 0.9 * moved)


def product_body(count, *refs):
    tokens, weights = refs[:9], refs[9 : 9 + count]
    keep, give, rows, columns, sems = refs[9 + count :]
    c, x, y = lax.axis_index("c"), lax.axis_index("x"), lax.axis_index("y")
    sources = []
    for piece, at, length in zip(tokens, (0, 96, 192, 288, 384, 432, 480, 576, 672), (96, 96, 96, 96, 48, 48, 96, 96, 96)):
        place = lax.rem(y + at // 96, 8) * 96 + at % 96
        sources.append((0, piece, rows.at[pl.ds(pl.multiple_of(place, 16), length)]))
    for j, source in enumerate(weights):
        if j < 4 or count == 8:
            lanes = pl.ds(pl.multiple_of(128 * lax.rem(x + j % 4, 4), 128), 128)
            sources.append((j // 4, source, columns.at[j // 4, :, lanes]))
        else:
            for at in range(4):
                sources.append((1, source.at[at], columns.at[1, :, pl.ds(128 * at, 128)]))
    copies = []
    for i, (stage, source, target) in enumerate(sources):
        copy = pltpu.make_async_copy(source, target, sems.at[i])
        copy.start()
        copies.append((stage, copy))
    for kind in range(2):
        for at, copy in copies:
            if at == kind:
                copy.wait()
        for pair in range(2):
            span = slice(256 * pair, 256 * pair + 256)
            for half in range(2):
                total = jnp.dot(rows[384 * half : 384 * half + 384], columns[kind, :, span], preferred_element_type=F32)
                for s in range(4):
                    low, high = total[96 * s : 96 * s + 48], total[96 * s + 48 : 96 * s + 96]
                    keep[kind, 4 * half + s, :, span] = jnp.where(c == 0, low, high).astype(BF)
                    give[kind, 4 * half + s, :, span] = jnp.where(c == 0, high, low).astype(BF)


def product(tokens, weights):
    return call(
        functools.partial(product_body, len(weights)),
        [*tokens, *weights],
        [like((2, 8, 48, 512), BF)] * 2,
        True,
        [pltpu.VMEM((768, 2048), BF), pltpu.VMEM((2, 2048, 512), BF), pltpu.SemaphoreType.DMA((17,))],
    )


def gated_body(keep, got, hidden):
    for x in range(4):
        columns = slice(128 * x, 128 * x + 128)
        g = keep[0, :, :, columns].astype(F32) + got[0, :, :, columns].astype(F32)
        u = keep[1, :, :, columns].astype(F32) + got[1, :, :, columns].astype(F32)
        hidden[x] = (g / (1.0 + jnp.exp(-g)) * u).astype(BF)


def per_device(tokens, gate_weight, pseudo_grad, anchor, momentum):
    c = lax.axis_index("c")

    grad = pseudo_grad.reshape(2, 2, 1024, 128)
    pick = lax.dynamic_index_in_dim(grad, 1 - c, 1, keepdims=False)
    got = flip(pick, "c")
    *parts, half_done, mine, other = call(
        prepare_body,
        [grad, got, anchor, momentum],
        [like((2, ROWS, 128), BF)] * PARTS + [like((1024, 128), F32)] * 3,
    )
    back = flip(parts[0], "zh")
    tokens = after(tokens, pick)
    cut = jnp.transpose(tokens[0].reshape(8, 2, 2, 1024), (2, 0, 1, 3)).reshape(2, 1, 8, 2048)
    cut = jnp.broadcast_to(cut, (2, 6, 8, 2048)).reshape(12, 8, 2048)
    six = lax.all_to_all(cut, ("c", "z"), 0, 0).reshape(96, 2048)
    six = after(six, parts[0])
    f1, b1 = shift(six, "y", 1), shift(six, "y", -1)
    f2, b2 = shift(f1, "y", 1), shift(b1, "y", -1)
    (up,) = call(functools.partial(update_body, 0), [back, half_done, other], [like((2, 1024, 128), BF)])
    ups = [up.reshape(2048, 128)]
    ups += [shift(ups[0], "x", -j) for j in (1, 2, 3)]
    f2, b2 = after(f2, up), after(b2, up)
    own = lax.dynamic_index_in_dim(gate_weight.reshape(2, 2, 1024, 128), c, 1, keepdims=False).reshape(2048, 128)
    gates = [own] + [shift(own, "x", -j) for j in (1, 2, 3)]
    f3, b3 = shift(f2, "y", 1), shift(b2, "y", -1)
    f3, b3, *gates = lax.optimization_barrier((f3, b3, *gates))
    f4, b4 = shift(f3[:48], "y", 1), shift(b3[48:], "y", -1)
    keep, give = product([six, b1, b2, b3, f4, b4, f3, f2, f1], [*gates, *ups])
    (hidden,) = call(gated_body, [keep, flip(give, "c")], [like((4, 8, 48, 128), BF)])
    hidden = lax.all_to_all(hidden, "x", 0, 0)
    hidden = jnp.transpose(hidden.reshape(4, 8, 6, 8, 128), (2, 0, 1, 3, 4)).reshape(1, 1536, 128)
    new_anchor, new_momentum = call(outer_body, [back, mine, anchor, momentum], [like((1024, 128), F32)] * 2)
    return new_anchor, new_momentum, hidden


def solution(mesh):
    fine = Mesh(mesh.devices.reshape(tuple(SIZES.values())), AXES)
    rep, fsdp = ("zh", "c"), ("z", "x", "y")
    return jax.shard_map(
        lambda t, g, p, a, m: per_device(t, g, p[0], a, m),
        mesh=fine,
        in_specs=(P(rep, fsdp, None), P(None, fsdp), P(rep, None, fsdp), P(rep, fsdp), P(rep, fsdp)),
        out_specs=(P(rep, fsdp), P(rep, fsdp), P(rep, None, fsdp)),
        check_vma=False,
    )
```

```python
import functools

import jax
import jax.numpy as jnp
from jax import lax
from jax.experimental import pallas as pl
from jax.experimental.pallas import tpu as pltpu
from jax.sharding import Mesh, PartitionSpec as P

SIZES = {"zh": 2, "c": 2, "z": 6, "x": 4, "y": 8}
AXES = tuple(SIZES)
BF, F32 = jnp.bfloat16, jnp.float32
MIB = 1024 * 1024
PARTS = 1
ROWS = 1024 // PARTS


def shift(value, axis, by):
    n = SIZES[axis]
    return lax.ppermute(value, axis, [(i, (i + by) % n) for i in range(n)])


def flip(value, axis):
    return lax.ppermute(value, axis, [(0, 1), (1, 0)])


def along(value, hops):
    pairs = []
    for zh in range(2):
        for c in range(2):
            for z in range(6):
                to = (6 * zh + z + (hops if c == 0 else -hops)) % 12
                pairs.append(((2 * zh + c) * 6 + z, (2 * (to // 6) + c) * 6 + to % 6))
    return lax.ppermute(value, ("zh", "c", "z"), pairs)


def after(value, *others):
    return lax.optimization_barrier((value, *others))[0]


def whole(a):
    return pl.BlockSpec(a.shape, lambda i: (0,) * len(a.shape))


def like(shape, dtype):
    return jax.ShapeDtypeStruct(shape, dtype)


def call(body, arrays, outs, held=False, scratch=()):
    return pl.pallas_call(
        body,
        out_shape=outs,
        grid=(1,),
        in_specs=[pl.BlockSpec(memory_space=pl.ANY) if held else whole(a) for a in arrays],
        out_specs=[whole(o) for o in outs],
        scratch_shapes=list(scratch),
        compiler_params=pltpu.CompilerParams(vmem_limit_bytes=60 * MIB),
        cost_estimate=pl.CostEstimate(flops=0, bytes_accessed=1024, transcendentals=0),
    )(*arrays)


def prepare_body(grad, got, anchor, momentum, *outs):
    parts, (half_done, mine, other) = outs[:PARTS], outs[PARTS:]
    zh, c = lax.axis_index("zh"), lax.axis_index("c")
    s = grad[zh, c].astype(F32) + got[zh].astype(F32)
    o = grad[1 - zh, c].astype(F32) + got[1 - zh].astype(F32)
    v = (anchor[...] - 0.567 * momentum[...]) - 0.3325 * s
    mine[...] = s
    other[...] = o
    half_done[...] = v
    for part, ref in enumerate(parts):
        rows = slice(ROWS * part, ROWS * part + ROWS)
        ref[0] = v[rows].astype(BF)
        ref[1] = o[rows].astype(BF)


def update_body(part, back, half_done, other, up):
    zh = lax.axis_index("zh")
    rows = pl.ds(ROWS * part, ROWS)
    here = (half_done[rows] - 0.3325 * back[1].astype(F32)).astype(BF)
    there = (back[0].astype(F32) - 0.3325 * other[rows]).astype(BF)
    for x in range(4):
        up[x, zh] = here
        up[x, 1 - zh] = there


def outer_body(*refs):
    backs, (mine, anchor, momentum, new_anchor, new_momentum) = refs[:PARTS], refs[PARTS:]
    for part, ref in enumerate(backs):
        rows = pl.ds(ROWS * part, ROWS)
        mean_delta = (mine[rows] + ref[1].astype(F32)) * 0.25
        moved = 0.9 * momentum[rows] + mean_delta
        new_momentum[rows] = moved
        new_anchor[rows] = anchor[rows] - 0.7 * (mean_delta + 0.9 * moved)


def product_body(*refs):
    tokens, weights = refs[:9], refs[9:11]
    keep, give, rows, columns, sems = refs[11:]
    c, y = lax.axis_index("c"), lax.axis_index("y")
    sources = []
    for piece, at, length in zip(tokens, (0, 96, 192, 288, 384, 432, 480, 576, 672), (96, 96, 96, 96, 48, 48, 96, 96, 96)):
        place = lax.rem(y + at // 96, 8) * 96 + at % 96
        sources.append((0, piece, rows.at[pl.ds(pl.multiple_of(place, 16), length)]))
    for kind in range(2):
        for x in range(4):
            target = columns.at[kind, :, pl.ds(128 * x, 128)]
            sources.append((2 * kind + x // 2, weights[kind].at[x], target))
    copies = []
    for i, (stage, source, target) in enumerate(sources):
        copy = pltpu.make_async_copy(source, target, sems.at[i])
        copy.start()
        copies.append((stage, copy))
    for stage in range(4):
        for at, copy in copies:
            if at == stage:
                copy.wait()
        kind, pair = stage // 2, stage % 2
        span = slice(256 * pair, 256 * pair + 256)
        for half in range(2):
            total = jnp.dot(rows[384 * half : 384 * half + 384], columns[kind, :, span], preferred_element_type=F32)
            for s in range(4):
                mixed = total[96 * s : 96 * s + 96].reshape(6, 2, 8, 256)
                low, high = mixed[:, 0].reshape(48, 256), mixed[:, 1].reshape(48, 256)
                keep[kind, 4 * half + s, :, span] = jnp.where(c == 0, low, high).astype(BF)
                give[kind, 4 * half + s, :, span] = jnp.where(c == 0, high, low).astype(BF)


def product(tokens, gate, up):
    return call(
        product_body,
        [*tokens, gate, up],
        [like((2, 8, 48, 512), BF)] * 2,
        True,
        [pltpu.VMEM((768, 2048), BF), pltpu.VMEM((2, 2048, 512), BF), pltpu.SemaphoreType.DMA((17,))],
    )


def gated_body(keep, got, hidden):
    for x in range(4):
        columns = slice(128 * x, 128 * x + 128)
        g = keep[0, :, :, columns].astype(F32) + got[0, :, :, columns].astype(F32)
        u = keep[1, :, :, columns].astype(F32) + got[1, :, :, columns].astype(F32)
        hidden[x] = (g / (1.0 + jnp.exp(-g)) * u).astype(BF)


def per_device(tokens, gate_weight, pseudo_grad, anchor, momentum):
    c = lax.axis_index("c")

    z = lax.axis_index("z")
    own = lax.dynamic_index_in_dim(gate_weight.reshape(2, 2, 1024, 128), c, 1, keepdims=False).reshape(1, 2048, 128)
    own = jnp.broadcast_to(own, (4, 2048, 128))
    gate_all = lax.all_to_all(own, "x", 0, 0)

    grad = pseudo_grad.reshape(2, 2, 1024, 128)
    got = flip(lax.dynamic_index_in_dim(grad, 1 - c, 1, keepdims=False), "c")
    *parts, half_done, mine, other = call(
        prepare_body,
        [grad, got, anchor, momentum],
        [like((2, ROWS, 128), BF)] * PARTS + [like((1024, 128), F32)] * 3,
    )
    back = along(along(parts[0], 5), 1)

    tok = tokens[0].reshape(8, 2, 2, 1024)
    kept = lax.dynamic_index_in_dim(tok, c, 2, keepdims=False)
    away = flip(lax.dynamic_index_in_dim(tok, 1 - c, 2, keepdims=False), "c")
    tok = jnp.where(c == 0, jnp.stack([kept, away]), jnp.stack([away, kept])).reshape(16, 2048)
    beside = lax.ppermute(tok, "z", [(i, i ^ 1) for i in range(6)])
    two = jnp.where(z % 2 == 0, jnp.stack([tok, beside]), jnp.stack([beside, tok]))
    two = after(two, parts[0])
    three = jnp.stack([two, shift(two, "z", -2), shift(two, "z", 2)] * 2)
    six = lax.dynamic_slice_in_dim(three, (3 - z // 2) % 3, 3, 0).reshape(96, 2048)
    f1, b1 = shift(six, "y", 1), shift(six, "y", -1)
    f2, b2 = shift(f1, "y", 1), shift(b1, "y", -1)
    f2, b2, back, gate_all = lax.optimization_barrier((f2, b2, back, gate_all))
    (up,) = call(functools.partial(update_body, 0), [back, half_done, other], [like((4, 2, 1024, 128), BF)])
    up_all = lax.all_to_all(up.reshape(4, 2048, 128), "x", 0, 0)
    f3, b3 = shift(f2, "y", 1), shift(b2, "y", -1)
    f4, b4 = shift(f2[:48], "y", 2), shift(b2[48:], "y", -2)
    keep, give = product([six, b1, b2, b3, f4, b4, f3, f2, f1], gate_all, up_all)
    (hidden,) = call(gated_body, [keep, flip(give, "c")], [like((4, 8, 48, 128), BF)])
    hidden = lax.all_to_all(hidden, "x", 0, 0)
    hidden = jnp.transpose(hidden.reshape(4, 8, 6, 8, 128), (2, 0, 1, 3, 4)).reshape(1, 1536, 128)
    new_anchor, new_momentum = call(outer_body, [back, mine, anchor, momentum], [like((1024, 128), F32)] * 2)
    return new_anchor, new_momentum, hidden


def solution(mesh):
    fine = Mesh(mesh.devices.reshape(tuple(SIZES.values())), AXES)
    rep, fsdp = ("zh", "c"), ("z", "x", "y")
    return jax.shard_map(
        lambda t, g, p, a, m: per_device(t, g, p[0], a, m),
        mesh=fine,
        in_specs=(P(rep, fsdp, None), P(None, fsdp), P(rep, None, fsdp), P(rep, fsdp), P(rep, fsdp)),
        out_specs=(P(rep, fsdp), P(rep, fsdp), P(rep, None, fsdp)),
        check_vma=False,
    )
```

```python
import functools

import jax
import jax.numpy as jnp
from jax import lax
from jax.experimental import pallas as pl
from jax.experimental.pallas import tpu as pltpu
from jax.sharding import Mesh, PartitionSpec as P

SIZES = {"zh": 2, "c": 2, "z": 6, "x": 4, "y": 8}
AXES = tuple(SIZES)
BF, F32 = jnp.bfloat16, jnp.float32
MIB = 1024 * 1024
PARTS = 1
ROWS = 1024 // PARTS


def shift(value, axis, by):
    n = SIZES[axis]
    return lax.ppermute(value, axis, [(i, (i + by) % n) for i in range(n)])


def flip(value, axis):
    return lax.ppermute(value, axis, [(0, 1), (1, 0)])


def along(value, hops):
    pairs = []
    for zh in range(2):
        for c in range(2):
            for z in range(6):
                to = (6 * zh + z + (hops if c == 0 else -hops)) % 12
                pairs.append(((2 * zh + c) * 6 + z, (2 * (to // 6) + c) * 6 + to % 6))
    return lax.ppermute(value, ("zh", "c", "z"), pairs)


def after(value, *others):
    return lax.optimization_barrier((value, *others))[0]


def whole(a):
    return pl.BlockSpec(a.shape, lambda i: (0,) * len(a.shape))


def like(shape, dtype):
    return jax.ShapeDtypeStruct(shape, dtype)


def call(body, arrays, outs, held=False, scratch=()):
    return pl.pallas_call(
        body,
        out_shape=outs,
        grid=(1,),
        in_specs=[pl.BlockSpec(memory_space=pl.ANY) if held else whole(a) for a in arrays],
        out_specs=[whole(o) for o in outs],
        scratch_shapes=list(scratch),
        compiler_params=pltpu.CompilerParams(vmem_limit_bytes=60 * MIB),
        cost_estimate=pl.CostEstimate(flops=0, bytes_accessed=1024, transcendentals=0),
    )(*arrays)


def prepare_body(grad, got, anchor, momentum, *outs):
    parts, (half_done, mine, other) = outs[:PARTS], outs[PARTS:]
    zh, c = lax.axis_index("zh"), lax.axis_index("c")
    s = grad[zh, c].astype(F32) + got[zh].astype(F32)
    o = grad[1 - zh, c].astype(F32) + got[1 - zh].astype(F32)
    v = (anchor[...] - 0.567 * momentum[...]) - 0.3325 * s
    mine[...] = s
    other[...] = o
    half_done[...] = v
    for part, ref in enumerate(parts):
        rows = slice(ROWS * part, ROWS * part + ROWS)
        ref[0] = v[rows].astype(BF)
        ref[1] = o[rows].astype(BF)


def update_body(part, back, half_done, other, up):
    zh = lax.axis_index("zh")
    rows = pl.ds(ROWS * part, ROWS)
    here = (half_done[rows] - 0.3325 * back[1].astype(F32)).astype(BF)
    there = (back[0].astype(F32) - 0.3325 * other[rows]).astype(BF)
    up[zh] = here
    up[1 - zh] = there


def outer_body(*refs):
    backs, (mine, anchor, momentum, new_anchor, new_momentum) = refs[:PARTS], refs[PARTS:]
    for part, ref in enumerate(backs):
        rows = pl.ds(ROWS * part, ROWS)
        mean_delta = (mine[rows] + ref[1].astype(F32)) * 0.25
        moved = 0.9 * momentum[rows] + mean_delta
        new_momentum[rows] = moved
        new_anchor[rows] = anchor[rows] - 0.7 * (mean_delta + 0.9 * moved)


def product_body(count, *refs):
    tokens, weights = refs[:9], refs[9 : 9 + count]
    keep, give, rows, columns, sems = refs[9 + count :]
    c, x, y = lax.axis_index("c"), lax.axis_index("x"), lax.axis_index("y")
    sources = []
    for piece, at, length in zip(tokens, (0, 96, 192, 288, 384, 432, 480, 576, 672), (96, 96, 96, 96, 48, 48, 96, 96, 96)):
        place = lax.rem(y + at // 96, 8) * 96 + at % 96
        sources.append((0, piece, rows.at[pl.ds(pl.multiple_of(place, 16), length)]))
    for j, source in enumerate(weights):
        if j < 4 or count == 8:
            lanes = pl.ds(pl.multiple_of(128 * lax.rem(x + j % 4, 4), 128), 128)
            sources.append((j // 4, source, columns.at[j // 4, :, lanes]))
        else:
            for at in range(4):
                sources.append((1, source.at[at], columns.at[1, :, pl.ds(128 * at, 128)]))
    copies = []
    for i, (stage, source, target) in enumerate(sources):
        copy = pltpu.make_async_copy(source, target, sems.at[i])
        copy.start()
        copies.append((stage, copy))
    for kind in range(2):
        for at, copy in copies:
            if at == kind:
                copy.wait()
        for pair in range(2):
            span = slice(256 * pair, 256 * pair + 256)
            for half in range(2):
                total = jnp.dot(rows[384 * half : 384 * half + 384], columns[kind, :, span], preferred_element_type=F32)
                for s in range(4):
                    low, high = total[96 * s : 96 * s + 48], total[96 * s + 48 : 96 * s + 96]
                    keep[kind, 4 * half + s, :, span] = jnp.where(c == 0, low, high).astype(BF)
                    give[kind, 4 * half + s, :, span] = jnp.where(c == 0, high, low).astype(BF)


def product(tokens, weights):
    return call(
        functools.partial(product_body, len(weights)),
        [*tokens, *weights],
        [like((2, 8, 48, 512), BF)] * 2,
        True,
        [pltpu.VMEM((768, 2048), BF), pltpu.VMEM((2, 2048, 512), BF), pltpu.SemaphoreType.DMA((17,))],
    )


def gated_body(keep, got, hidden):
    for x in range(4):
        columns = slice(128 * x, 128 * x + 128)
        g = keep[0, :, :, columns].astype(F32) + got[0, :, :, columns].astype(F32)
        u = keep[1, :, :, columns].astype(F32) + got[1, :, :, columns].astype(F32)
        hidden[x] = (g / (1.0 + jnp.exp(-g)) * u).astype(BF)


def per_device(tokens, gate_weight, pseudo_grad, anchor, momentum):
    c = lax.axis_index("c")

    grad = pseudo_grad.reshape(2, 2, 1024, 128)
    pick = lax.dynamic_index_in_dim(grad, 1 - c, 1, keepdims=False)
    got = flip(pick, "c")
    *parts, half_done, mine, other = call(
        prepare_body,
        [grad, got, anchor, momentum],
        [like((2, ROWS, 128), BF)] * PARTS + [like((1024, 128), F32)] * 3,
    )
    back = along(along(parts[0], 1), 5)
    tokens = after(tokens, pick)
    cut = jnp.transpose(tokens[0].reshape(8, 2, 2, 1024), (2, 0, 1, 3)).reshape(2, 1, 8, 2048)
    cut = jnp.broadcast_to(cut, (2, 6, 8, 2048)).reshape(12, 8, 2048)
    six = lax.all_to_all(cut, ("c", "z"), 0, 0).reshape(96, 2048)
    six = after(six, parts[0])
    f1, b1 = shift(six, "y", 1), shift(six, "y", -1)
    f2, b2 = shift(f1, "y", 1), shift(b1, "y", -1)
    (up,) = call(functools.partial(update_body, 0), [back, half_done, other], [like((2, 1024, 128), BF)])
    ups = [up.reshape(2048, 128)]
    ups += [shift(ups[0], "x", -j) for j in (1, 2, 3)]
    f2, b2 = after(f2, up), after(b2, up)
    own = lax.dynamic_index_in_dim(gate_weight.reshape(2, 2, 1024, 128), c, 1, keepdims=False).reshape(2048, 128)
    gates = [own] + [shift(own, "x", -j) for j in (1, 2, 3)]
    f3, b3 = shift(f2, "y", 1), shift(b2, "y", -1)
    f3, b3, *gates = lax.optimization_barrier((f3, b3, *gates))
    f4, b4 = shift(f3[:48], "y", 1), shift(b3[48:], "y", -1)
    keep, give = product([six, b1, b2, b3, f4, b4, f3, f2, f1], [*gates, *ups])
    (hidden,) = call(gated_body, [keep, flip(give, "c")], [like((4, 8, 48, 128), BF)])
    hidden = lax.all_to_all(hidden, "x", 0, 0)
    hidden = jnp.transpose(hidden.reshape(4, 8, 6, 8, 128), (2, 0, 1, 3, 4)).reshape(1, 1536, 128)
    new_anchor, new_momentum = call(outer_body, [back, mine, anchor, momentum], [like((1024, 128), F32)] * 2)
    return new_anchor, new_momentum, hidden


def solution(mesh):
    fine = Mesh(mesh.devices.reshape(tuple(SIZES.values())), AXES)
    rep, fsdp = ("zh", "c"), ("z", "x", "y")
    return jax.shard_map(
        lambda t, g, p, a, m: per_device(t, g, p[0], a, m),
        mesh=fine,
        in_specs=(P(rep, fsdp, None), P(None, fsdp), P(rep, None, fsdp), P(rep, fsdp), P(rep, fsdp)),
        out_specs=(P(rep, fsdp), P(rep, fsdp), P(rep, None, fsdp)),
        check_vma=False,
    )
```
